32 devices in a mesh: groups: 2 (over x), mp: 16 (over z, y, core).
Axes of the slice: x: 2, y: 2, z: 4, core: 2. Of those that a mesh axis runs over, the one named last changes fastest.
Arguments:
- tokens: bfloat16 [2048, 8192], P('groups', 'mp'), parts along dimension 0, may hold values from -6 to 6
- up_blocks: bfloat16 [128, 8, 64, 512], P('mp'), may hold values from -0.25 to 0.25
- up_left: bfloat16 [8192, 256], P('mp'), may hold values from -0.0625 to 0.0625
- up_right: bfloat16 [256, 65536], P(None, 'mp'), may hold values from -0.375 to 0.375
- down_blocks: bfloat16 [128, 8, 512, 64], P('mp'), may hold values from -0.09375 to 0.09375
- down_left: bfloat16 [65536, 256], P('mp'), may hold values from -0.0234375 to 0.0234375
- down_right: bfloat16 [256, 8192], P(None, 'mp'), may hold values from -0.375 to 0.375
- cotangent: bfloat16 [2048, 8192], P('groups', 'mp'), parts along dimension 0, may hold values from -6 to 6
Outputs:
- output: bfloat16 [2048, 8192], P('groups', 'mp'), parts along dimension 0
- grad_tokens: bfloat16 [2048, 8192], P('groups', 'mp'), parts along dimension 0
- grad_up_blocks: float32 [256, 8, 64, 512], P(('groups', 'mp')), parts along dimension 0
- grad_up_left: float32 [16384, 256], P(('groups', 'mp')), parts along dimension 0
- grad_up_right: float32 [512, 65536], P('groups', 'mp'), parts along dimension 0
- grad_down_blocks: float32 [256, 8, 512, 64], P(('groups', 'mp')), parts along dimension 0
- grad_down_left: float32 [131072, 256], P(('groups', 'mp')), parts along dimension 0
- grad_down_right: float32 [512, 8192], P('groups', 'mp'), parts along dimension 0
The draws below stay inside these ranges and needn't reach their ends.
There are 2 independent parts, one for each index of `groups`. The reference program is written for one: setup_inputs(seed, part) draws one part's arguments, and reference() takes and returns one part's arrays. A program takes and returns all parts, laid end to end along the dimension named above; an argument that names none is the same for every part. Nothing has to cross between parts.
All inputs are finite; a program needn't handle non-finite values.
Results may differ from the reference program's by a relative error of at most 0.0061.
Values may be sent and summed in bfloat16 or wider, within the bound.
A program may use at most 512 MiB of HBM per device.

```python
import jax
import jax.numpy as jnp
import numpy as np

D = 8192
H = 65536
GRID = 128
LEVELS = 7
RANK = 256
TOK = 1024
BROWS = 64
BCOLS = 512


def levels(own_key, extent, shards, smallest, top_value):
    gain = 1.0
    for position, parts in shards:
        heights = jax.random.uniform(jax.random.fold_in(jax.random.fold_in(own_key, 6), position), (parts,), jnp.float32, smallest / len(shards), top_value / len(shards))
        gain = gain * jnp.repeat(jnp.exp(heights), extent[position] // parts).reshape((-1,) + (1,) * (len(extent) - 1 - position))
    return gain


def bell_draw(stream_key, shape, deviation, reach, split=(), kind=jnp.bfloat16):
    drawn = jax.random.normal(stream_key, shape, jnp.float32) * deviation
    if len(split) > 0:
        drawn = levels(stream_key, shape, split, -0.22, 0.18) * drawn
    return jnp.clip(drawn, min=-reach, max=reach).astype(kind)


def setup_inputs(seed: int = 0, part: int = 0) -> dict:
    key_of = jax.random.split(jax.random.key(seed), 9)
    own_keys = jax.random.split(jax.random.fold_in(key_of[8], part), 9)
    return {
        "tokens": bell_draw(own_keys[0], (TOK, D), 1.0, 6.0, ((1, 16),)),
        "up_blocks": bell_draw(key_of[1], (GRID, LEVELS + 1, BROWS, BCOLS), ((LEVELS + 1) * BROWS) ** -0.5, 0.25, ((0, 16),)),
        "up_left": bell_draw(key_of[2], (D, RANK), D ** -0.5, 0.0625, ((0, 16),)),
        "up_right": bell_draw(key_of[3], (RANK, H), RANK ** -0.5, 0.375, ((1, 16),)),
        "down_blocks": bell_draw(key_of[4], (GRID, LEVELS + 1, BCOLS, BROWS), ((LEVELS + 1) * BCOLS) ** -0.5, 0.09375, ((0, 16),)),
        "down_left": bell_draw(key_of[5], (H, RANK), H ** -0.5, 0.0234375, ((0, 16),)),
        "down_right": bell_draw(key_of[6], (RANK, D), RANK ** -0.5, 0.375, ((1, 16),)),
        "cotangent": bell_draw(own_keys[7], (TOK, D), 1.0, 6.0, ((1, 16),)),
    }


def gelu_value(field):
    inner = 0.7978845608 * (field + 0.044715 * field * field * field)
    return 0.5 * field * (1.0 + jnp.tanh(inner))


def gelu_slope(field):
    tangent = jnp.tanh(0.7978845608 * (field + 0.044715 * field * field * field))
    return 0.5 * (1.0 + tangent) + 0.5 * field * (1.0 - tangent * tangent) * 0.7978845608 * (1.0 + 3.0 * 0.044715 * field * field)


def reference(tokens, up_blocks, up_left, up_right, down_blocks, down_left, down_right, cotangent):
    tok_rows = tokens.shape[0]
    partner_lists = [np.arange(GRID)] + [np.arange(GRID) ^ (1 << level) for level in range(LEVELS)]
    inputs_blocks = tokens.astype(jnp.float32).reshape(tok_rows, GRID, BROWS)
    cot_blocks = cotangent.astype(jnp.float32).reshape(tok_rows, GRID, BROWS)
    low_a = jnp.dot(tokens, up_left, preferred_element_type=jnp.float32).astype(jnp.bfloat16)
    hidden = jnp.zeros((tok_rows, GRID, BCOLS), jnp.float32)
    for slot_index in range(LEVELS + 1):
        hidden = hidden + jnp.einsum('tjd,jde->tje', inputs_blocks[:, partner_lists[slot_index]], up_blocks[:, slot_index].astype(jnp.float32))
    hidden = hidden.reshape(tok_rows, H) + jnp.dot(low_a, up_right, preferred_element_type=jnp.float32)
    act = gelu_value(hidden).astype(jnp.bfloat16)
    act_blocks = act.astype(jnp.float32).reshape(tok_rows, GRID, BCOLS)
    low_b = jnp.dot(act, down_left, preferred_element_type=jnp.float32).astype(jnp.bfloat16)
    mixed = jnp.zeros((tok_rows, GRID, BROWS), jnp.float32)
    for slot_index in range(LEVELS + 1):
        terms = jnp.einsum('tje,jed->tjd', act_blocks, down_blocks[:, slot_index].astype(jnp.float32))
        mixed = mixed + terms[:, partner_lists[slot_index]]
    output = (mixed.reshape(tok_rows, D) + jnp.dot(low_b, down_right, preferred_element_type=jnp.float32)).astype(jnp.bfloat16)

    grad_down_right = jnp.einsum('tr,td->rd', low_b.astype(jnp.float32), cotangent.astype(jnp.float32))
    low_db = jnp.dot(cotangent, down_right.T, preferred_element_type=jnp.float32).astype(jnp.bfloat16)
    grad_act = jnp.zeros((tok_rows, GRID, BCOLS), jnp.float32)
    down_grads = []
    for slot_index in range(LEVELS + 1):
        gathered = cot_blocks[:, partner_lists[slot_index]]
        grad_act = grad_act + jnp.einsum('tjd,jed->tje', gathered, down_blocks[:, slot_index].astype(jnp.float32))
        down_grads.append(jnp.einsum('tje,tjd->jed', act_blocks, gathered))
    grad_down_blocks = jnp.stack(down_grads, axis=1)
    grad_down_left = jnp.einsum('th,tr->hr', act.astype(jnp.float32), low_db.astype(jnp.float32))
    grad_act = grad_act.reshape(tok_rows, H) + jnp.dot(low_db, down_left.T, preferred_element_type=jnp.float32)
    grad_hidden = (grad_act * gelu_slope(hidden)).astype(jnp.bfloat16)
    grad_up_right = jnp.einsum('tr,th->rh', low_a.astype(jnp.float32), grad_hidden.astype(jnp.float32))
    low_da = jnp.dot(grad_hidden, up_right.T, preferred_element_type=jnp.float32).astype(jnp.bfloat16)
    hidden_blocks = grad_hidden.astype(jnp.float32).reshape(tok_rows, GRID, BCOLS)
    back_mixed = jnp.zeros((tok_rows, GRID, BROWS), jnp.float32)
    up_grads = []
    for slot_index in range(LEVELS + 1):
        up_grads.append(jnp.einsum('tjd,tje->jde', inputs_blocks[:, partner_lists[slot_index]], hidden_blocks))
        terms = jnp.einsum('tje,jde->tjd', hidden_blocks, up_blocks[:, slot_index].astype(jnp.float32))
        back_mixed = back_mixed + terms[:, partner_lists[slot_index]]
    grad_up_blocks = jnp.stack(up_grads, axis=1)
    grad_up_left = jnp.einsum('td,tr->dr', tokens.astype(jnp.float32), low_da.astype(jnp.float32))
    grad_tokens = (back_mixed.reshape(tok_rows, D) + jnp.dot(low_da, up_left.T, preferred_element_type=jnp.float32)).astype(jnp.bfloat16)
    return (output, grad_tokens, grad_up_blocks, grad_up_left, grad_up_right, grad_down_blocks, grad_down_left, grad_down_right)
```

```python
import functools

import jax
import jax.numpy as jnp
from jax import lax
from jax.experimental import pallas as pl
from jax.experimental.pallas import tpu as pltpu
from jax.sharding import PartitionSpec as P

CHUNKS = 2
TILE = 256
VMEM_BYTES = 48 * 1024 * 1024


def partner(block, axis, stride):
    count = lax.axis_size(axis)
    route = []
    for low in range(count):
        high = low | 1 << stride
        if high != low and high < count:
            route += [(low, high), (high, low)]
    return lax.ppermute(block, axis, route)


def gelu_both(field):
    square = field * field
    tangent = jnp.tanh(field * (0.7978845608 + 0.7978845608 * 0.044715 * square))
    half = 0.5 + 0.5 * tangent
    slope = half + 0.5 * field * (1.0 - tangent * tangent) * (
        0.7978845608 + 0.7978845608 * 3.0 * 0.044715 * square
    )
    return field * half, slope


def mul(left, right, left_dim, right_dim):
    return lax.dot_general(
        left, right, (((left_dim,), (right_dim,)), ((), ())), preferred_element_type=jnp.float32
    )


def middle_kernel(local_bits, remote_bits, *refs):
    slots = 1 + local_bits + remote_bits
    pieces = refs[:slots]
    up_ref, down_ref, right_ref, left_ref, low_ref = refs[slots : slots + 5]
    act_ref, grad_ref, near_ref, sums_ref = refs[slots + 5 : slots + 9]
    fars = refs[slots + 9 :]
    column = pl.program_id(0)

    @pl.when(column == 0)
    def _():
        near_ref[...] = jnp.zeros_like(near_ref)
        sums_ref[...] = jnp.zeros_like(sums_ref)

    rank = right_ref.shape[0]
    rows = pieces[0].shape[2]
    width = pieces[0].shape[3]
    tile = min(TILE, width)
    up = up_ref[0]
    down = down_ref[0]
    right = right_ref[...]
    left = left_ref[...]
    for start in range(0, width, tile):
        span = pl.ds(start, tile)
        x = jnp.concatenate([piece[0, 0, :, span] for piece in pieces], axis=0)
        c = jnp.concatenate([piece[1, 0, :, span] for piece in pieces], axis=0)
        hidden = mul(up, x, 0, 0) + mul(right, low_ref[:rank, span], 0, 0)
        grad_act = mul(down, c, 0, 0) + mul(left, low_ref[rank:, span], 1, 0)
        value, slope = gelu_both(hidden)
        act = value.astype(jnp.bfloat16)
        grad = (grad_act * slope).astype(jnp.bfloat16)
        act_ref[0, :, span] = act
        grad_ref[0, :, span] = grad
        sums_ref[:rank, span] += mul(left, act, 0, 0)
        sums_ref[rank:, span] += mul(right, grad, 1, 0)
        for side, (weight, field) in enumerate(((down, act), (up, grad))):
            terms = mul(weight, field, 1, 0)
            for slot in range(slots):
                term = terms[slot * rows : (slot + 1) * rows]
                if slot <= local_bits:
                    target = column ^ ((1 << slot) >> 1)
                    near_ref[side, target, :, span] += term
                else:
                    fars[slot - 1 - local_bits][side, 0, :, span] = term.astype(jnp.bfloat16)


def grad_kernel(chunks, slots, *refs):
    pieces = [refs[part * slots : (part + 1) * slots] for part in range(chunks)]
    rest = refs[chunks * slots :]
    acts, grads, lows = rest[:chunks], rest[chunks : 2 * chunks], rest[2 * chunks : 3 * chunks]
    up_ref, down_ref, right_ref, left_ref = rest[3 * chunks :]
    rank = right_ref.shape[0]

    def total(terms):
        return functools.reduce(lambda one, two: one + two, terms)

    up_ref[0] = total(
        mul(jnp.concatenate([piece[0, 0] for piece in pieces[part]], axis=0), grads[part][0], 1, 1)
        for part in range(chunks)
    )
    down_ref[0] = total(
        mul(jnp.concatenate([piece[1, 0] for piece in pieces[part]], axis=0), acts[part][0], 1, 1)
        for part in range(chunks)
    )
    right_ref[...] = total(
        mul(lows[part][:rank], grads[part][0], 1, 1) for part in range(chunks)
    )
    left_ref[...] = total(
        mul(acts[part][0], lows[part][rank:], 1, 1) for part in range(chunks)
    )


def local(tokens, up_blocks, up_left, up_right, down_blocks, down_left, down_right, cotangent):
    tok_rows, feat_width = tokens.shape
    col_count, slots, rows, col_block = up_blocks.shape
    rank = up_left.shape[1]
    local_bits = col_count.bit_length() - 1
    remote_bits = lax.axis_size("mp").bit_length() - 1
    deep = slots * rows
    part = tok_rows // CHUNKS
    up = up_blocks.reshape(col_count, deep, col_block)
    down = down_blocks.swapaxes(2, 3).reshape(col_count, deep, col_block)
    both = jnp.stack([tokens.T, cotangent.T])
    mine = [
        both[:, :, start : start + part].reshape(2, col_count, rows, part)
        for start in range(0, tok_rows, part)
    ]

    def shared_sum(total):
        piece = lax.psum_scatter(total, "mp", scatter_dimension=0, tiled=True)
        return lax.all_gather(piece.astype(jnp.bfloat16), "mp", axis=0, tiled=True)

    low = shared_sum(
        jnp.concatenate(
            [
                jnp.einsum("dr,dt->rt", up_left, both[0], preferred_element_type=jnp.float32),
                jnp.einsum("rd,dt->rt", down_right, both[1], preferred_element_type=jnp.float32),
            ]
        )
    )
    lows = [low[:, start : start + part] for start in range(0, tok_rows, part)]

    own_specs = [
        pl.BlockSpec((2, 1, rows, part), lambda j, m=(1 << slot) >> 1: (0, j ^ m, 0, 0))
        for slot in range(1 + local_bits)
    ]
    far_spec = pl.BlockSpec((2, 1, rows, part), lambda j: (0, j, 0, 0))
    piece_specs = own_specs + [far_spec] * remote_bits
    block_spec = pl.BlockSpec((1, deep, col_block), lambda j: (j, 0, 0))
    field_spec = pl.BlockSpec((1, col_block, part), lambda j: (j, 0, 0))
    right_spec = pl.BlockSpec((rank, col_block), lambda j: (0, j))
    left_spec = pl.BlockSpec((col_block, rank), lambda j: (j, 0))
    low_spec = pl.BlockSpec((2 * rank, part), lambda j: (0, 0))
    field = jax.ShapeDtypeStruct((col_count, col_block, part), jnp.bfloat16)
    hidden_units = col_count * col_block
    params = pltpu.CompilerParams(vmem_limit_bytes=VMEM_BYTES)
    flops = 2 * tok_rows * hidden_units * (deep + rank)
    middle = pl.pallas_call(
        functools.partial(middle_kernel, local_bits, remote_bits),
        grid=(col_count,),
        in_specs=piece_specs + [block_spec, block_spec, right_spec, left_spec, low_spec],
        out_specs=[
            field_spec,
            field_spec,
            pl.BlockSpec((2, col_count, rows, part), lambda j: (0, 0, 0, 0)),
            low_spec,
        ]
        + [far_spec] * remote_bits,
        out_shape=[
            field,
            field,
            jax.ShapeDtypeStruct((2, col_count, rows, part), jnp.float32),
            jax.ShapeDtypeStruct((2 * rank, part), jnp.float32),
        ]
        + [jax.ShapeDtypeStruct((2, col_count, rows, part), jnp.bfloat16)] * remote_bits,
        compiler_params=params,
        cost_estimate=pl.CostEstimate(
            flops=4 * flops // CHUNKS,
            bytes_accessed=64 * hidden_units * part // 8,
            transcendentals=hidden_units * part,
        ),
    )
    pieces, fields, grads, nears, sums, far_terms = [], [], [], [], [], []
    for index in range(CHUNKS):
        far = [partner(mine[index], "mp", level) for level in reversed(range(remote_bits))][::-1]
        pieces.append([mine[index]] * (1 + local_bits) + far)
    for index in range(CHUNKS):
        act, grad, near, total, *terms = middle(
            *pieces[index], up, down, up_right, down_left, lows[index]
        )
        far_terms.append(
            [partner(terms[level], "mp", level) for level in reversed(range(remote_bits))]
        )
        sums.append(shared_sum(total))
        fields.append(act)
        grads.append(grad)
        nears.append(near)

    grad_up, grad_down, grad_up_right, grad_down_left = pl.pallas_call(
        functools.partial(grad_kernel, CHUNKS, slots),
        grid=(col_count,),
        in_specs=piece_specs * CHUNKS + [field_spec] * (2 * CHUNKS) + [low_spec] * CHUNKS,
        out_specs=[block_spec, block_spec, right_spec, left_spec],
        out_shape=[
            jax.ShapeDtypeStruct((col_count, deep, col_block), jnp.float32),
            jax.ShapeDtypeStruct((col_count, deep, col_block), jnp.float32),
            jax.ShapeDtypeStruct(up_right.shape, jnp.float32),
            jax.ShapeDtypeStruct(down_left.shape, jnp.float32),
        ],
        compiler_params=params,
        cost_estimate=pl.CostEstimate(
            flops=2 * flops, bytes_accessed=16 * hidden_units * tok_rows, transcendentals=0
        ),
    )(*[piece for group in pieces for piece in group], *fields, *grads, *lows)

    results = []
    for index in range(CHUNKS):
        mixed = nears[index]
        for term in far_terms[index]:
            mixed = mixed + term.astype(jnp.float32)
        mixed = mixed.reshape(2, feat_width, part)
        back = jnp.stack(
            [
                jnp.einsum(
                    "rd,rt->dt", down_right, sums[index][:rank], preferred_element_type=jnp.float32
                ),
                jnp.einsum(
                    "dr,rt->dt", up_left, sums[index][rank:], preferred_element_type=jnp.float32
                ),
            ]
        )
        results.append((mixed + back).astype(jnp.bfloat16))
    result = jnp.concatenate(results, axis=2)
    total = jnp.concatenate(sums, axis=1)
    grad_down_right = jnp.einsum(
        "rt,dt->rd", total[:rank], both[1], preferred_element_type=jnp.float32
    )
    grad_up_left = jnp.einsum(
        "dt,rt->dr", both[0], total[rank:], preferred_element_type=jnp.float32
    )
    return (
        result[0].T,
        result[1].T,
        grad_up.reshape(up_blocks.shape),
        grad_up_left,
        grad_up_right,
        grad_down.reshape(col_count, slots, rows, col_block).swapaxes(2, 3),
        grad_down_left,
        grad_down_right,
    )


def solution(mesh):
    return jax.shard_map(
        local,
        mesh=mesh,
        in_specs=(
            P("groups", "mp"),
            P("mp", None, None, None),
            P("mp", None),
            P(None, "mp"),
            P("mp", None, None, None),
            P("mp", None),
            P(None, "mp"),
            P("groups", "mp"),
        ),
        out_specs=(
            P("groups", "mp"),
            P("groups", "mp"),
            P(("groups", "mp"), None, None, None),
            P(("groups", "mp"), None),
            P("groups", "mp"),
            P(("groups", "mp"), None, None, None),
            P(("groups", "mp"), None),
            P("groups", "mp"),
        ),
        check_vma=False,
    )
```

```python
import functools

import jax
import jax.numpy as jnp
from jax import lax
from jax.experimental import pallas as pl
from jax.experimental.pallas import tpu as pltpu
from jax.sharding import PartitionSpec as P

CHUNKS = 2
TILE = 256
VMEM_BYTES = 48 * 1024 * 1024


def partner(block, axis, stride):
    count = lax.axis_size(axis)
    route = []
    for low in range(count):
        high = low | 1 << stride
        if high != low and high < count:
            route += [(low, high), (high, low)]
    return lax.ppermute(block, axis, route)


def gelu_both(field):
    square = field * field
    tangent = jnp.tanh(field * (0.7978845608 + 0.7978845608 * 0.044715 * square))
    half = 0.5 + 0.5 * tangent
    slope = half + 0.5 * field * (1.0 - tangent * tangent) * (
        0.7978845608 + 0.7978845608 * 3.0 * 0.044715 * square
    )
    return field * half, slope


def mul(left, right, left_dim, right_dim):
    return lax.dot_general(
        left, right, (((left_dim,), (right_dim,)), ((), ())), preferred_element_type=jnp.float32
    )


def middle_kernel(local_bits, remote_bits, *refs):
    slots = 1 + local_bits + remote_bits
    pieces = refs[:slots]
    up_ref, down_ref, right_ref, left_ref, low_ref = refs[slots : slots + 5]
    act_ref, grad_ref, near_ref, sums_ref = refs[slots + 5 : slots + 9]
    fars = refs[slots + 9 :]
    column = pl.program_id(0)

    @pl.when(column == 0)
    def _():
        near_ref[...] = jnp.zeros_like(near_ref)
        sums_ref[...] = jnp.zeros_like(sums_ref)

    rank = right_ref.shape[0]
    rows = pieces[0].shape[2]
    width = pieces[0].shape[3]
    tile = min(TILE, width)
    up = up_ref[0]
    down = down_ref[0]
    right = right_ref[...]
    left = left_ref[...]
    for start in range(0, width, tile):
        span = pl.ds(start, tile)
        x = jnp.concatenate([piece[0, 0, :, span] for piece in pieces], axis=0)
        c = jnp.concatenate([piece[1, 0, :, span] for piece in pieces], axis=0)
        hidden = mul(up, x, 0, 0) + mul(right, low_ref[:rank, span], 0, 0)
        grad_act = mul(down, c, 0, 0) + mul(left, low_ref[rank:, span], 1, 0)
        value, slope = gelu_both(hidden)
        act = value.astype(jnp.bfloat16)
        grad = (grad_act * slope).astype(jnp.bfloat16)
        act_ref[0, :, span] = act
        grad_ref[0, :, span] = grad
        sums_ref[:rank, span] += mul(left, act, 0, 0)
        sums_ref[rank:, span] += mul(right, grad, 1, 0)
        for side, (weight, field) in enumerate(((down, act), (up, grad))):
            terms = mul(weight, field, 1, 0)
            for slot in range(slots):
                term = terms[slot * rows : (slot + 1) * rows]
                if slot <= local_bits:
                    target = column ^ ((1 << slot) >> 1)
                    near_ref[side, target, :, span] += term
                else:
                    fars[slot - 1 - local_bits][side, 0, :, span] = term.astype(jnp.bfloat16)


def grad_kernel(chunks, slots, *refs):
    pieces = [refs[part * slots : (part + 1) * slots] for part in range(chunks)]
    rest = refs[chunks * slots :]
    acts, grads, lows = rest[:chunks], rest[chunks : 2 * chunks], rest[2 * chunks : 3 * chunks]
    up_ref, down_ref, right_ref, left_ref = rest[3 * chunks :]
    rank = right_ref.shape[0]

    def total(terms):
        return functools.reduce(lambda one, two: one + two, terms)

    up_ref[0] = total(
        mul(jnp.concatenate([piece[0, 0] for piece in pieces[part]], axis=0), grads[part][0], 1, 1)
        for part in range(chunks)
    )
    down_ref[0] = total(
        mul(jnp.concatenate([piece[1, 0] for piece in pieces[part]], axis=0), acts[part][0], 1, 1)
        for part in range(chunks)
    )
    right_ref[...] = total(
        mul(lows[part][:rank], grads[part][0], 1, 1) for part in range(chunks)
    )
    left_ref[...] = total(
        mul(acts[part][0], lows[part][rank:], 1, 1) for part in range(chunks)
    )


def local(tokens, up_blocks, up_left, up_right, down_blocks, down_left, down_right, cotangent):
    tok_rows, feat_width = tokens.shape
    col_count, slots, rows, col_block = up_blocks.shape
    rank = up_left.shape[1]
    local_bits = col_count.bit_length() - 1
    remote_bits = lax.axis_size("mp").bit_length() - 1
    deep = slots * rows
    part = tok_rows // CHUNKS
    up = up_blocks.reshape(col_count, deep, col_block)
    down = down_blocks.swapaxes(2, 3).reshape(col_count, deep, col_block)
    both = jnp.stack([tokens.T, cotangent.T])
    mine = [
        both[:, :, start : start + part].reshape(2, col_count, rows, part)
        for start in range(0, tok_rows, part)
    ]

    fars = [
        [partner(mine[index], "mp", level) for level in reversed(range(remote_bits))][::-1]
        for index in range(CHUNKS)
    ]

    def shared_sum(total, after=()):
        piece = lax.psum_scatter(total, "mp", scatter_dimension=0, tiled=True)
        for other in after:
            piece = piece + 0.0 * other[0, 0, :1, :1].astype(jnp.float32)
        return lax.all_gather(piece.astype(jnp.bfloat16), "mp", axis=0, tiled=True)

    low = shared_sum(
        jnp.concatenate(
            [
                jnp.einsum("dr,dt->rt", up_left, both[0], preferred_element_type=jnp.float32),
                jnp.einsum("rd,dt->rt", down_right, both[1], preferred_element_type=jnp.float32),
            ]
        ),
        fars[0],
    )
    lows = [low[:, start : start + part] for start in range(0, tok_rows, part)]

    own_specs = [
        pl.BlockSpec((2, 1, rows, part), lambda j, m=(1 << slot) >> 1: (0, j ^ m, 0, 0))
        for slot in range(1 + local_bits)
    ]
    far_spec = pl.BlockSpec((2, 1, rows, part), lambda j: (0, j, 0, 0))
    piece_specs = own_specs + [far_spec] * remote_bits
    block_spec = pl.BlockSpec((1, deep, col_block), lambda j: (j, 0, 0))
    field_spec = pl.BlockSpec((1, col_block, part), lambda j: (j, 0, 0))
    right_spec = pl.BlockSpec((rank, col_block), lambda j: (0, j))
    left_spec = pl.BlockSpec((col_block, rank), lambda j: (j, 0))
    low_spec = pl.BlockSpec((2 * rank, part), lambda j: (0, 0))
    field = jax.ShapeDtypeStruct((col_count, col_block, part), jnp.bfloat16)
    hidden_units = col_count * col_block
    params = pltpu.CompilerParams(vmem_limit_bytes=VMEM_BYTES)
    flops = 2 * tok_rows * hidden_units * (deep + rank)
    middle = pl.pallas_call(
        functools.partial(middle_kernel, local_bits, remote_bits),
        grid=(col_count,),
        in_specs=piece_specs + [block_spec, block_spec, right_spec, left_spec, low_spec],
        out_specs=[
            field_spec,
            field_spec,
            pl.BlockSpec((2, col_count, rows, part), lambda j: (0, 0, 0, 0)),
            low_spec,
        ]
        + [far_spec] * remote_bits,
        out_shape=[
            field,
            field,
            jax.ShapeDtypeStruct((2, col_count, rows, part), jnp.float32),
            jax.ShapeDtypeStruct((2 * rank, part), jnp.float32),
        ]
        + [jax.ShapeDtypeStruct((2, col_count, rows, part), jnp.bfloat16)] * remote_bits,
        compiler_params=params,
        cost_estimate=pl.CostEstimate(
            flops=4 * flops // CHUNKS,
            bytes_accessed=64 * hidden_units * part // 8,
            transcendentals=hidden_units * part,
        ),
    )
    pieces, fields, grads, nears, sums, far_terms = [], [], [], [], [], []
    for index in range(CHUNKS):
        pieces.append([mine[index]] * (1 + local_bits) + fars[index])
    for index in range(CHUNKS):
        act, grad, near, total, *terms = middle(
            *pieces[index], up, down, up_right, down_left, lows[index]
        )
        far_terms.append(
            [partner(terms[level], "mp", level) for level in reversed(range(remote_bits))]
        )
        sums.append(total)
        fields.append(act)
        grads.append(grad)
        nears.append(near)

    grad_up, grad_down, grad_up_right, grad_down_left = pl.pallas_call(
        functools.partial(grad_kernel, CHUNKS, slots),
        grid=(col_count,),
        in_specs=piece_specs * CHUNKS + [field_spec] * (2 * CHUNKS) + [low_spec] * CHUNKS,
        out_specs=[block_spec, block_spec, right_spec, left_spec],
        out_shape=[
            jax.ShapeDtypeStruct((col_count, deep, col_block), jnp.float32),
            jax.ShapeDtypeStruct((col_count, deep, col_block), jnp.float32),
            jax.ShapeDtypeStruct(up_right.shape, jnp.float32),
            jax.ShapeDtypeStruct(down_left.shape, jnp.float32),
        ],
        compiler_params=params,
        cost_estimate=pl.CostEstimate(
            flops=2 * flops, bytes_accessed=16 * hidden_units * tok_rows, transcendentals=0
        ),
    )(*[piece for group in pieces for piece in group], *fields, *grads, *lows)

    total = shared_sum(jnp.concatenate(sums, axis=1))
    sums = [total[:, start : start + part] for start in range(0, tok_rows, part)]
    results = []
    for index in range(CHUNKS):
        mixed = nears[index]
        for term in far_terms[index]:
            mixed = mixed + term.astype(jnp.float32)
        mixed = mixed.reshape(2, feat_width, part)
        back = jnp.stack(
            [
                jnp.einsum(
                    "rd,rt->dt", down_right, sums[index][:rank], preferred_element_type=jnp.float32
                ),
                jnp.einsum(
                    "dr,rt->dt", up_left, sums[index][rank:], preferred_element_type=jnp.float32
                ),
            ]
        )
        results.append((mixed + back).astype(jnp.bfloat16))
    result = jnp.concatenate(results, axis=2)
    grad_down_right = jnp.einsum(
        "rt,dt->rd", total[:rank], both[1], preferred_element_type=jnp.float32
    )
    grad_up_left = jnp.einsum(
        "dt,rt->dr", both[0], total[rank:], preferred_element_type=jnp.float32
    )
    return (
        result[0].T,
        result[1].T,
        grad_up.reshape(up_blocks.shape),
        grad_up_left,
        grad_up_right,
        grad_down.reshape(col_count, slots, rows, col_block).swapaxes(2, 3),
        grad_down_left,
        grad_down_right,
    )


def solution(mesh):
    return jax.shard_map(
        local,
        mesh=mesh,
        in_specs=(
            P("groups", "mp"),
            P("mp", None, None, None),
            P("mp", None),
            P(None, "mp"),
            P("mp", None, None, None),
            P("mp", None),
            P(None, "mp"),
            P("groups", "mp"),
        ),
        out_specs=(
            P("groups", "mp"),
            P("groups", "mp"),
            P(("groups", "mp"), None, None, None),
            P(("groups", "mp"), None),
            P("groups", "mp"),
            P(("groups", "mp"), None, None, None),
            P(("groups", "mp"), None),
            P("groups", "mp"),
        ),
        check_vma=False,
    )
```
